256 devices in a mesh: row: 8 (over x_hi, y), col: 32 (over z, x_lo, core).
Axes of the slice: x: 4 (x_hi: 2, x_lo: 2; x = x_hi * 2 + x_lo), y: 4, z: 8, core: 2. Of those that a mesh axis runs over, the one named last changes fastest.
Arguments:
- query_grads: bfloat16 [2, 8192, 28672], P(None, 'row', 'col'), may hold values from -6 to 6
- basis_in: bfloat16 [8192, 1024], P('row', 'col'), may hold values from -0.1875 to 0.1875
- basis_out: bfloat16 [28672, 1024], P('col', 'row'), may hold values from -0.03125 to 0.03125
- eig_in: float32 [1024], P('row'), may hold values from 0.1 to 1
- eig_out: float32 [1024], P('col'), may hold values from 0.1 to 1
- damping: float32 [1], replicated, may hold values from 0.02 to 0.2
Outputs:
- preconditioned: bfloat16 [2, 8192, 28672], P(None, 'row', 'col')
The draws below stay inside these ranges and needn't reach their ends.
All inputs are finite; a program needn't handle non-finite values.
Results may differ from the reference program's by a relative error of at most 0.023.
Values may be sent and summed in bfloat16 or wider, within the bound.
A program may use at most 128 MiB of HBM per device.

```python
import math
import jax
import jax.numpy as jnp
from jax import lax

D = 8192
F = 28672
Q = 2
KA = 1024
KS = 1024


def block_scale(stream_key, extent, split, smallest, top_value):
    def one(dim, parts):
        heights = jax.random.uniform(jax.random.fold_in(jax.random.fold_in(stream_key, 6), dim), (parts,), jnp.float32, smallest / len(split), top_value / len(split))
        return jnp.repeat(jnp.exp(heights), extent[dim] // parts).reshape((-1,) + (1,) * (len(extent) - dim - 1))

    factor_of = one(*split[0])
    for cut in split[1:]:
        factor_of = factor_of * one(*cut)
    return factor_of


def scatter_about(rng, extent, scale, bound, pieces=(), held_as=jnp.bfloat16):
    gain = block_scale(rng, extent, pieces, -0.22, 0.18) if pieces else 1.0
    values = jax.random.normal(rng, extent, jnp.float32) * scale * gain
    return jnp.minimum(jnp.maximum(values, -bound), bound).astype(held_as)


def setup_inputs(seed: int = 0) -> dict:
    key_list = jax.random.split(jax.random.key(seed), 7)
    return {
        "query_grads": scatter_about(key_list[0], (Q, D, F), 1.0, 6.0, ((1, 8), (2, 32))),
        "basis_in": scatter_about(key_list[1], (D, KA), KA ** -0.5, 0.1875, ((0, 8), (1, 32))),
        "basis_out": scatter_about(key_list[2], (F, KS), F ** -0.5, 0.03125, ((0, 32), (1, 8))),
        "eig_in": jnp.clip(jnp.exp(math.log(1.0) - 2.3025851 * jax.random.uniform(key_list[3], (KA,), jnp.float32) ** block_scale(key_list[3], (KA,), ((0, 8),), -0.2, 0.2)), 0.1, 1.0),
        "eig_out": jnp.clip(jnp.exp(math.log(1.0) - 2.3025851 * jax.random.uniform(key_list[4], (KS,), jnp.float32) ** block_scale(key_list[4], (KS,), ((0, 32),), -0.2, 0.2)), 0.1, 1.0),
        "damping": jnp.clip(jax.random.uniform(key_list[5], (1,), jnp.float32, 0.02, 0.2), 0.02, 0.2),
    }


def reference(query_grads, basis_in, basis_out, eig_in, eig_out, damping):
    denom = eig_in[:, None] * eig_out[None, :] + damping[0]
    out_float = basis_out.astype(jnp.float32)
    results = []
    for index in range(Q):
        grad_one = query_grads[index]
        half_left = jnp.dot(basis_in.T, grad_one, preferred_element_type=jnp.float32)
        rotated = jnp.dot(half_left, out_float, precision=lax.Precision.HIGHEST)
        scaled = (rotated / denom).astype(jnp.bfloat16)
        back_half = jnp.dot(scaled, basis_out.T, preferred_element_type=jnp.float32).astype(jnp.bfloat16)
        result = jnp.dot(basis_in, back_half, preferred_element_type=jnp.float32).astype(jnp.bfloat16)
        results.append(result)
    return jnp.stack(results, axis=0)
```

```python
import functools

import jax
import jax.numpy as jnp
from jax import lax
from jax.experimental import pallas as pl
from jax.experimental.pallas import tpu as pltpu
from jax.sharding import PartitionSpec as P

MESH = pl.DeviceIdType.MESH
BF = jnp.bfloat16
F32 = jnp.float32
NSEM = 160


def nt(a, b):
    return lax.dot_general(a, b, (((1,), (1,)), ((), ())), preferred_element_type=F32)


def nn(a, b):
    return lax.dot_general(a, b, (((1,), (0,)), ((), ())), preferred_element_type=F32)


def kernel(
    g_hbm, bi_in, bo_in, ei, eo, damp, out_hbm,
    g, bit, bot, yt, sibs, sibr, own, c1a, c1b, r1a, r1b, c2a, c2b, r2a, r2b, e, re, sc,
    st0, st1, bi0, bi1, acc, ob, ssem, rsem, lsem,
):
    r = lax.axis_index("row")
    c = lax.axis_index("col")
    xh, y, z, xl, k = r // 4, r % 4, c // 4, (c // 2) % 2, c % 2
    x = 2 * xh + xl

    def dev(x_, y_, z_, k_):
        return ((x_ // 2) * 4 + y_, z_ * 4 + (x_ % 2) * 2 + k_)

    xs = [(x + d) % 4 for d in (1, 2, 3)]
    ys = [(y + d) % 4 for d in (1, 2, 3)]
    zs = [(z + d) % 8 for d in range(1, 8)]
    xdev = [dev(v, y, z, k) for v in xs]
    ydev = [dev(x, v, z, k) for v in ys]
    zdev = [dev(x, y, v, k) for v in zs]
    sib = dev(x, y, z, 1 - k)
    xlp = dev(2 * xh + 1 - xl, y, z, k)
    xhp = xdev[1]

    sends = []
    counter = [0]

    def send(src, dst, to):
        i = counter[0]
        counter[0] += 1
        cp = pltpu.make_async_remote_copy(
            src_ref=src, dst_ref=dst, send_sem=ssem.at[i], recv_sem=rsem.at[i],
            device_id=to, device_id_type=MESH,
        )
        cp.start()
        sends.append(cp)
        return cp

    gcopy = pltpu.make_async_copy(g_hbm, g, lsem.at[0])
    gcopy.start()
    obo = [pltpu.make_async_copy(bo_in.at[i], bot.at[i, r], lsem.at[1 + i]) for i in range(2)]
    obi = pltpu.make_async_copy(bi_in, bit.at[z, xl, k], lsem.at[3])
    for cp in obo + [obi]:
        cp.start()

    barrier = pltpu.get_barrier_semaphore()
    partners = xdev + ydev + zdev + [sib]
    for p in partners:
        pl.semaphore_signal(barrier, inc=1, device_id=p, device_id_type=MESH)
    pl.semaphore_wait(barrier, len(partners))

    a_x = send(bo_in.at[0], bot.at[0, r], xhp)
    bi_ring = {}
    zr, zl = zdev[0], zdev[6]
    bi_ring[0, 0, 1] = send(bi_in, bit.at[z, xl, k], zr)
    bi_ring[1, 0, 1] = send(bi_in, bit.at[z, xl, k], zl)
    bi_x = send(bi_in, bit.at[z, xl, k], xlp)
    b_y = [send(bo_in.at[1], bot.at[1, r], p) for p in ydev]
    b_x0 = send(bo_in.at[1], bot.at[1, r], xhp)
    a_y = [send(bo_in.at[0], bot.at[0, r], p) for p in ydev]
    bi_sib = [send(bi_in, bit.at[z, xl, k], sib)]

    def xside(v):
        return (1 - xh) * 4 + v

    bi_x.wait_recv()
    blk = bit.at[z, 1 - xl, k]
    bi_ring[0, 1, 1] = send(blk, blk, zr)
    bi_ring[1, 1, 1] = send(blk, blk, zl)
    bi_sib.append(send(blk, blk, sib))
    a_x.wait_recv()
    blk = bot.at[0, xside(y)]
    a_xy = [send(blk, blk, p) for p in ydev]

    def ring_step(t):
        for b in range(2):
            for d in range(2):
                if (d, b, t) not in bi_ring:
                    continue
                bi_ring[d, b, t].wait_recv()
                zz = (z - t + 8) % 8 if d == 0 else (z + t) % 8
                xx = xl if b == 0 else 1 - xl
                blk = bit.at[zz, xx, k]
                if t < 3 or (t == 3 and b == d):
                    bi_ring[d, b, t + 1] = send(blk, blk, zr if d == 0 else zl)
                bi_sib.append(send(blk, blk, sib))

    ring_step(1)
    b_xy = []
    for i in (0, 2, 1):
        b_y[i].wait_recv()
        blk = bot.at[1, xh * 4 + (y + 3 - i) % 4]
        b_xy.append(send(blk, blk, xhp))
    for cp in obo + [obi, gcopy]:
        cp.wait()
    for cp in a_y:
        cp.wait_recv()
    ring_step(2)

    def y_dot(kk, h):
        lhs = bot[kk, pl.ds(4 * h, 4)].reshape(256, 896)
        for q in range(2):
            for n in range(2):
                yt[kk, h, q, :, pl.ds(512 * n, 512)] = nt(lhs, g[q, pl.ds(512 * n, 512), :]).astype(BF)

    y_dot(0, xh)
    ring_step(3)
    y_dot(1, xh)
    b_x0.wait_recv()
    for cp in b_xy:
        cp.wait_recv()
    for cp in a_xy:
        cp.wait_recv()
    ring_step(4)
    y_dot(0, 1 - xh)
    y_dot(1, 1 - xh)
    for cp in bi_sib:
        cp.wait_recv()

    chunks = [(0, 0), (1, 0), (0, 1), (1, 1)]

    def bit_cols(n):
        return bit[pl.ds(2 * n, 2)].reshape(256, 1024)

    def partial(i):
        q, h = chunks[i]
        lhs = yt[1 - k, h, q]
        for n in range(4):
            sibs[i, :, pl.ds(256 * n, 256)] = nt(lhs, bit_cols(n)).astype(BF)
        cp = send(sibs.at[i], sibr.at[i], sib)
        lhs = yt[k, h, q]
        for n in range(4):
            own[i, :, pl.ds(256 * n, 256)] = nt(lhs, bit_cols(n))
        return cp

    def first(i, cp):
        q, h = chunks[i]
        cp.wait_recv()
        for zz in range(4):
            for xx in range(2):
                rows = pl.ds(64 * zz + 32 * xx, 32)
                v = (own[i, rows, :] + sibr[i, rows, :].astype(F32)).astype(BF)
                if q == 0:
                    for hh in range(2):
                        c1a[h, 2 * hh + xx, pl.ds(32 * zz, 32), :] = v[:, 512 * hh : 512 * hh + 512]
                else:
                    for hh in range(2):
                        for yy in range(4):
                            lo = 512 * hh + 128 * yy
                            c1b[h, yy, pl.ds(128 * (2 * hh + xx) + 32 * zz, 32), :] = v[:, lo : lo + 128]
        if q == 0:
            return [send(c1a.at[h, xs[d]], r1a.at[h, d], xdev[d]) for d in (1, 0, 2)]
        return [send(c1b.at[h, ys[d]], r1b.at[h, d], ydev[d]) for d in (1, 0, 2)]

    def second(i, cps):
        q, h = chunks[i]
        for cp in cps:
            cp.wait_recv()
        if q == 0:
            for zz in range(4):
                rows = pl.ds(32 * zz, 32)
                v = c1a[h, x, rows, :].astype(F32)
                for d in range(3):
                    v = v + r1a[h, d, rows, :].astype(F32)
                v = v.astype(BF)
                for yy in range(4):
                    c2a[h, yy, rows, :] = v[:, 128 * yy : 128 * yy + 128]
            return [send(c2a.at[h, ys[d]], r2a.at[h, d], ydev[d]) for d in (1, 0, 2)]
        for xx in range(4):
            rows = pl.ds(128 * xx, 128)
            v = c1b[h, y, rows, :].astype(F32)
            for d in range(3):
                v = v + r1b[h, d, rows, :].astype(F32)
            c2b[h, xx] = v.astype(BF)
        return [send(c2b.at[h, xs[d]], r2b.at[h, d], xdev[d]) for d in (1, 0, 2)]

    def third(i, cps):
        q, h = chunks[i]
        for cp in cps:
            cp.wait_recv()
        if q == 0:
            v = c2a[h, y].astype(F32)
            for d in range(3):
                v = v + r2a[h, d].astype(F32)
        else:
            v = c2b[h, x].astype(F32)
            for d in range(3):
                v = v + r2b[h, d].astype(F32)
        v = v.astype(BF)
        for zz in range(4):
            e[4 * h + zz, q] = v[32 * zz : 32 * zz + 32, :]

    p0 = partial(0)
    p1 = partial(1)
    f0 = first(0, p0)
    p2 = partial(2)
    f1 = first(1, p1)
    p3 = partial(3)
    f2 = first(2, p2)
    f3 = first(3, p3)

    eye = (
        lax.broadcasted_iota(jnp.int32, (256, 256), 0) == lax.broadcasted_iota(jnp.int32, (256, 256), 1)
    ).astype(F32).astype(BF)
    for i in range(4):
        for n in range(4):
            v = nt(eye, bit[pl.ds(2 * n, 2), :, :, :, pl.ds(256 * i, 256)].reshape(256, 256)).astype(BF)
            rows = pl.ds(256 * i, 256)
            bi0[n // 2, rows, pl.ds(256 * (n % 2), 256)] = v
            for b in range(2):
                rr = 2 * n + b
                bi1[rr % 4, rows, pl.ds(128 * (rr // 4), 128)] = v[:, 128 * b : 128 * b + 128]

    s0 = second(0, f0)
    s1 = second(1, f1)
    s2 = second(2, f2)
    s3 = second(3, f3)
    third(0, s0)
    third(1, s1)
    third(2, s2)
    third(3, s3)
    zsend = [send(e.at[zs[d]], re.at[d], zdev[d]) for d in (3, 2, 4, 1, 5, 0, 6)]
    denom = eo[...] * ei[...] + damp[0]
    v = e[z].astype(F32)
    for cp in zsend:
        cp.wait_recv()
    for d in range(7):
        v = v + re[d].astype(F32)
    sc[...] = (v / denom[None]).astype(BF)

    yl = pl.ds(pl.multiple_of(128 * y, 128), 128)
    hl = pl.ds(pl.multiple_of(128 * xh, 128), 128)
    g0 = [send(sc.at[0], st0.at[xh, k, z, xl, :, yl], zdev[d]) for d in (3, 2, 4, 1, 5, 0, 6)]
    g1 = [send(sc.at[1], st1.at[y, k, z, xl, :, hl], zdev[d]) for d in (3, 2, 4, 1, 5, 0, 6)]
    st0[xh, k, z, xl, :, yl] = sc[0]
    st1[y, k, z, xl, :, hl] = sc[1]
    for cp in g0:
        cp.wait_recv()
    blk = st0.at[xh, k, :, xl, :, yl]
    g0 = [send(blk, blk, ydev[d]) for d in (1, 0, 2)]
    for cp in g1:
        cp.wait_recv()
    blk = st1.at[y, k, :, xl, :, hl]
    g1 = [send(blk, blk, xdev[d]) for d in (1, 0, 2)]

    def reg(q, h, v, kk):
        if q == 0:
            return st0.at[v // 2, kk, pl.ds(4 * h, 4), v % 2]
        return st1.at[v, kk, pl.ds(4 * h, 4)]

    heavy = {}
    cores = {}
    for cp in g0:
        cp.wait_recv()
    for h in range(2):
        blk = reg(0, h, x, k)
        heavy[0, h] = [send(blk, blk, xdev[d]) for d in (1, 0, 2)]
    for cp in g1:
        cp.wait_recv()
    for h in range(2):
        blk = reg(1, h, y, k)
        heavy[1, h] = [send(blk, blk, ydev[d]) for d in (1, 0, 2)]
    for h in range(2):
        for q in range(2):
            blk = reg(q, h, x if q == 0 else y, k)
            cores[q, h] = [send(blk, blk, sib)]

    def spread(q, h):
        at = x if q == 0 else y
        for i, d in enumerate((1, 0, 2)):
            heavy[q, h][i].wait_recv()
            blk = reg(q, h, (at + 3 - d) % 4, k)
            cores[q, h].append(send(blk, blk, sib))

    outs = []

    def finish(q, h):
        for cp in cores[q, h]:
            cp.wait_recv()

        def step(m):
            rows = pl.ds(pl.multiple_of(256 * m, 256), 256)
            o = None
            for kk in range(2):
                if q == 0:
                    v = nt(bi0[0, rows, :], st0[0, kk, pl.ds(4 * h, 4)].reshape(256, 512))
                    v = v + nt(bi0[1, rows, :], st0[1, kk, pl.ds(4 * h, 4)].reshape(256, 512))
                else:
                    v = nt(bi1[0, rows, :], st1[0, kk, pl.ds(4 * h, 4)].reshape(256, 256))
                    for n in range(1, 4):
                        v = v + nt(bi1[n, rows, :], st1[n, kk, pl.ds(4 * h, 4)].reshape(256, 256))
                t = nn(v.astype(BF), bot[kk, pl.ds(4 * h, 4)].reshape(256, 896))
                o = t if o is None else o + t
            if h == 0:
                acc[q, rows, :] = o
            else:
                ob[q, rows, :] = (acc[q, rows, :] + o).astype(BF)

        pl.loop(0, 4)(step)
        if h == 1:
            cp = pltpu.make_async_copy(ob.at[q], out_hbm.at[q], lsem.at[4 + q])
            cp.start()
            outs.append(cp)

    spread(0, 0)
    spread(1, 0)
    finish(0, 0)
    finish(1, 0)
    spread(0, 1)
    spread(1, 1)
    finish(0, 1)
    finish(1, 1)
    for cp in sends:
        cp.wait_send()
    for cp in outs:
        cp.wait()
    assert counter[0] <= NSEM, counter[0]


def body(query_grads, basis_in, basis_out, eig_in, eig_out, damping):
    bi = basis_in.T
    bo = basis_out.T.reshape(2, 2, 32, 896).transpose(1, 0, 2, 3).reshape(2, 64, 896)
    vm = pl.BlockSpec(memory_space=pltpu.VMEM)
    hbm = pl.BlockSpec(memory_space=pl.ANY)
    return pl.pallas_call(
        kernel,
        out_shape=jax.ShapeDtypeStruct((2, 1024, 896), BF),
        in_specs=[hbm, vm, vm, vm, vm, pl.BlockSpec(memory_space=pltpu.SMEM)],
        out_specs=hbm,
        scratch_shapes=[
            pltpu.VMEM((2, 1024, 896), BF),
            pltpu.VMEM((8, 2, 2, 32, 1024), BF),
            pltpu.VMEM((2, 8, 64, 896), BF),
            pltpu.VMEM((2, 2, 2, 256, 1024), BF),
            pltpu.VMEM((4, 256, 1024), BF),
            pltpu.VMEM((4, 256, 1024), BF),
            pltpu.VMEM((4, 256, 1024), F32),
            pltpu.VMEM((2, 4, 128, 512), BF),
            pltpu.VMEM((2, 4, 512, 128), BF),
            pltpu.VMEM((2, 3, 128, 512), BF),
            pltpu.VMEM((2, 3, 512, 128), BF),
            pltpu.VMEM((2, 4, 128, 128), BF),
            pltpu.VMEM((2, 4, 128, 128), BF),
            pltpu.VMEM((2, 3, 128, 128), BF),
            pltpu.VMEM((2, 3, 128, 128), BF),
            pltpu.VMEM((8, 2, 32, 128), BF),
            pltpu.VMEM((7, 2, 32, 128), BF),
            pltpu.VMEM((2, 32, 128), BF),
            pltpu.VMEM((2, 2, 8, 2, 32, 512), BF),
            pltpu.VMEM((4, 2, 8, 2, 32, 256), BF),
            pltpu.VMEM((2, 1024, 512), BF),
            pltpu.VMEM((4, 1024, 256), BF),
            pltpu.VMEM((2, 1024, 896), F32),
            pltpu.VMEM((2, 1024, 896), BF),
            pltpu.SemaphoreType.DMA((NSEM,)),
            pltpu.SemaphoreType.DMA((NSEM,)),
            pltpu.SemaphoreType.DMA((6,)),
        ],
        compiler_params=pltpu.CompilerParams(
            collective_id=1, has_side_effects=True, vmem_limit_bytes=60 * 1024 * 1024
        ),
        cost_estimate=pl.CostEstimate(flops=17_000_000_000, bytes_accessed=8_000_000, transcendentals=0),
    )(query_grads, bi, bo, eig_in.reshape(1, 128), eig_out.reshape(32, 1), damping)


def solution(mesh):
    return jax.shard_map(
        body,
        mesh=mesh,
        in_specs=(P(None, "row", "col"), P("row", "col"), P("col", "row"), P("row"), P("col"), P()),
        out_specs=P(None, "row", "col"),
        check_vma=False,
    )
```

```python
import functools

import jax
import jax.numpy as jnp
from jax import lax
from jax.experimental import pallas as pl
from jax.experimental.pallas import tpu as pltpu
from jax.sharding import PartitionSpec as P

MESH = pl.DeviceIdType.MESH
BF = jnp.bfloat16
F32 = jnp.float32
NSEM = 200
VMEM = 49152 * 1024


def nt(a, b):
    return lax.dot_general(a, b, (((1,), (1,)), ((), ())), preferred_element_type=F32)


def nn(a, b):
    return lax.dot_general(a, b, (((1,), (0,)), ((), ())), preferred_element_type=F32)


def kernel(
    g_hbm, bi_hbm, bo_hbm, ei_hbm, eo_hbm, damp_hbm, out_hbm,
    g, bov, bit, bot, yt, sibs, sibr, own, c1a, c1b, r1a, r1b, c2a, c2b, r2a, r2b, e, re, zg,
    st0, st1, bi0, bi1, acc, ob, ei, eo, damp, ssem, rsem, lsem, zsem,
):
    r = lax.axis_index("row")
    c = lax.axis_index("col")
    xh, y, z, xl, k = r // 4, r % 4, c // 4, (c // 2) % 2, c % 2
    x = 2 * xh + xl

    def dev(x_, y_, z_, k_):
        return ((x_ // 2) * 4 + y_, z_ * 4 + (x_ % 2) * 2 + k_)

    xs = [(x + d) % 4 for d in (1, 2, 3)]
    ys = [(y + d) % 4 for d in (1, 2, 3)]
    xdev = [dev(v, y, z, k) for v in xs]
    ydev = [dev(x, v, z, k) for v in ys]
    zdev = [None] + [dev(x, y, (z + d) % 8, k) for d in range(1, 8)]
    sib = dev(x, y, z, 1 - k)
    xlp = dev(2 * xh + 1 - xl, y, z, k)
    xhp = xdev[1]

    sends = []
    counter = [0]

    def send(src, dst, to):
        i = counter[0]
        counter[0] += 1
        cp = pltpu.make_async_remote_copy(
            src_ref=src, dst_ref=dst, send_sem=ssem.at[i], recv_sem=rsem.at[i],
            device_id=to, device_id_type=MESH,
        )
        cp.start()
        sends.append(cp)
        return cp

    def load(i, src, dst):
        cp = pltpu.make_async_copy(src, dst, lsem.at[i])
        cp.start()
        return cp

    barrier = pltpu.get_barrier_semaphore()
    partners = [xdev[1], xdev[0], xdev[2], ydev[0], ydev[2], zdev[1], zdev[7], sib]
    for p in partners:
        pl.semaphore_signal(barrier, inc=1, device_id=p, device_id_type=MESH)
    lbo = load(0, bo_hbm, bov)
    lbi = load(1, bi_hbm, bit.at[z, xl, k])
    later = [load(2, ei_hbm, ei), load(3, eo_hbm, eo), load(4, damp_hbm, damp)]
    lg = load(5, g_hbm, g)

    lbo.wait()
    to = lax.broadcasted_iota(jnp.int32, (128, 128), 0)
    at = (to // 32 % 2) * 64 + (to // 64) * 32 + to % 32
    perm = (at == lax.broadcasted_iota(jnp.int32, (128, 128), 1)).astype(F32).astype(BF)
    v = nt(perm, bov[...]).astype(BF)
    bot[0, r] = v[:64]
    bot[1, r] = v[64:]
    lbi.wait()
    pl.semaphore_wait(barrier, len(partners))

    yup, ydn = ydev[0], ydev[2]
    zr, zl = zdev[1], zdev[7]
    me = bit.at[z, xl, k]
    ring = {(0, 0, 1): send(me, me, zr), (1, 0, 1): send(me, me, zl)}
    bi_x = send(me, me, xlp)
    blk = bot.at[0, r]
    a_x = send(blk, blk, xhp)
    near = {}
    blk = bot.at[1, r]
    near[1, "own"] = [send(blk, blk, yup), send(blk, blk, ydn)]
    bi_sib = [send(me, me, sib)]

    def pass_y(kk, side, hh):
        for cp in near[kk, side]:
            cp.wait_recv()
        lo = bot.at[kk, 4 * hh + (y + 3) % 4, pl.ds(0, 32)]
        hi = bot.at[kk, 4 * hh + (y + 1) % 4, pl.ds(32, 32)]
        near[kk, side, 2] = [send(lo, lo, yup), send(hi, hi, ydn)]

    def ring_step(t, b):
        for d in range(2):
            if (d, b, t) not in ring:
                continue
            ring[d, b, t].wait_recv()
            zz = (z - t + 8) % 8 if d == 0 else (z + t) % 8
            blk = bit.at[zz, xl if b == 0 else 1 - xl, k]
            if t < 3 or (t == 3 and b == d):
                ring[d, b, t + 1] = send(blk, blk, zr if d == 0 else zl)
            bi_sib.append(send(blk, blk, sib))

    def y_dot(kk, h, q):
        lhs = bot[kk, pl.ds(4 * h, 4)].reshape(256, 896)
        for n in range(2):
            yt[kk, h, q, :, pl.ds(512 * n, 512)] = nt(lhs, g[q, pl.ds(512 * n, 512), :]).astype(BF)

    bi_x.wait_recv()
    blk = bit.at[z, 1 - xl, k]
    ring[0, 1, 1] = send(blk, blk, zr)
    ring[1, 1, 1] = send(blk, blk, zl)
    blk = bot.at[1, r]
    b_x = [send(blk, blk, xhp)]
    blk = bit.at[z, 1 - xl, k]
    bi_sib.append(send(blk, blk, sib))
    pass_y(1, "own", xh)
    for v in ((y + 3) % 4, (y + 1) % 4):
        blk = bot.at[1, 4 * xh + v]
        b_x.append(send(blk, blk, xhp))
    blk = bot.at[0, r]
    near[0, "own"] = [send(blk, blk, yup), send(blk, blk, ydn)]
    ring_step(1, 0)
    ring_step(1, 1)
    ring_step(2, 0)
    pass_y(0, "own", xh)
    ring_step(2, 1)
    ring_step(3, 0)
    a_x.wait_recv()
    blk = bot.at[0, 4 * (1 - xh) + y]
    near[0, "far"] = [send(blk, blk, yup), send(blk, blk, ydn)]
    for i, cp in enumerate(near[1, "own", 2]):
        cp.wait_recv()
        blk = bot.at[1, 4 * xh + (y + 2) % 4, pl.ds(32 * i, 32)]
        b_x.append(send(blk, blk, xhp))
    lg.wait()
    y_dot(1, xh, 0)
    y_dot(1, xh, 1)
    ring_step(3, 1)
    pass_y(0, "far", 1 - xh)
    ring_step(4, 0)
    for cp in near[0, "own", 2]:
        cp.wait_recv()
    y_dot(0, xh, 0)
    ring_step(4, 1)
    y_dot(0, xh, 1)
    for cp in near[0, "far", 2]:
        cp.wait_recv()
    y_dot(0, 1 - xh, 0)
    y_dot(0, 1 - xh, 1)
    for cp in b_x:
        cp.wait_recv()
    y_dot(1, 1 - xh, 0)
    y_dot(1, 1 - xh, 1)
    for cp in bi_sib:
        cp.wait_recv()

    chunks = [(0, 0), (1, 0), (0, 1), (1, 1)]

    def bit_cols(n):
        return bit[pl.ds(2 * n, 2)].reshape(256, 1024)

    def partial(i):
        q, h = chunks[i]
        lhs = yt[1 - k, h, q]
        for n in range(4):
            sibs[i, :, pl.ds(256 * n, 256)] = nt(lhs, bit_cols(n)).astype(BF)
        cp = send(sibs.at[i], sibr.at[i], sib)
        lhs = yt[k, h, q]
        for n in range(4):
            own[i, :, pl.ds(256 * n, 256)] = nt(lhs, bit_cols(n))
        return cp

    def first(i, cp):
        q, h = chunks[i]
        cp.wait_recv()
        for zz in range(4):
            for xx in range(2):
                rows = pl.ds(64 * zz + 32 * xx, 32)
                v = (own[i, rows, :] + sibr[i, rows, :].astype(F32)).astype(BF)
                if q == 0:
                    for hh in range(2):
                        c1a[h, 2 * hh + xx, pl.ds(32 * zz, 32), :] = v[:, 512 * hh : 512 * hh + 512]
                else:
                    for hh in range(2):
                        for yy in range(4):
                            lo = 512 * hh + 128 * yy
                            c1b[h, yy, pl.ds(128 * (2 * hh + xx) + 32 * zz, 32), :] = v[:, lo : lo + 128]
        return relay(i, 0)

    def relay(i, step):
        q, h = chunks[i]
        src, dst, n, at = (c1a, r1a, 64, x) if q == 0 else (c1b, r1b, 256, y)
        far, up, down = (at + 2) % 4, (at + 1) % 4, (at + 3) % 4
        pu, _, pd = xdev if q == 0 else ydev
        lo, hi = pl.ds(0, n), pl.ds(n, n)
        if step == 0:
            return [
                send(src.at[h, far, lo], dst.at[h, 0, lo], pu),
                send(src.at[h, far, hi], dst.at[h, 0, hi], pd),
                send(src.at[h, up, hi], dst.at[h, 1, hi], pu),
                send(src.at[h, down, lo], dst.at[h, 2, lo], pd),
            ]
        cps = firsts[i]
        cps[0].wait_recv()
        src[h, up, lo, :] = (src[h, up, lo, :].astype(F32) + dst[h, 0, lo, :].astype(F32)).astype(BF)
        a = send(src.at[h, up, lo], dst.at[h, 1, lo], pu)
        cps[1].wait_recv()
        src[h, down, hi, :] = (src[h, down, hi, :].astype(F32) + dst[h, 0, hi, :].astype(F32)).astype(BF)
        b = send(src.at[h, down, hi], dst.at[h, 2, hi], pd)
        return [cps[2], cps[3], a, b]

    def second(i, cps):
        q, h = chunks[i]
        for cp in cps:
            cp.wait_recv()
        if q == 0:
            for zz in range(4):
                rows = pl.ds(32 * zz, 32)
                v = c1a[h, x, rows, :].astype(F32)
                for d in range(1, 3):
                    v = v + r1a[h, d, rows, :].astype(F32)
                v = v.astype(BF)
                for yy in range(4):
                    c2a[h, yy, rows, :] = v[:, 128 * yy : 128 * yy + 128]
            return [send(c2a.at[h, ys[d]], r2a.at[h, d], ydev[d]) for d in (1, 0, 2)]
        for xx in range(4):
            rows = pl.ds(128 * xx, 128)
            v = c1b[h, y, rows, :].astype(F32)
            for d in range(1, 3):
                v = v + r1b[h, d, rows, :].astype(F32)
            c2b[h, xx] = v.astype(BF)
        return [send(c2b.at[h, xs[d]], r2b.at[h, d], xdev[d]) for d in (1, 0, 2)]

    def third(i, cps):
        q, h = chunks[i]
        for cp in cps:
            cp.wait_recv()
        if q == 0:
            v = c2a[h, y].astype(F32)
            for d in range(3):
                v = v + r2a[h, d].astype(F32)
        else:
            v = c2b[h, x].astype(F32)
            for d in range(3):
                v = v + r2b[h, d].astype(F32)
        v = v.astype(BF)
        for zz in range(4):
            e[4 * h + zz, q] = v[32 * zz : 32 * zz + 32, :]

    def sum_z(h, i):
        zt = 4 * h + i
        d = (zt - z + 8) % 8
        cp = pltpu.make_async_remote_copy(
            src_ref=e.at[zt], dst_ref=re.at[d], send_sem=zsem.at[0, zt], recv_sem=zsem.at[1, d],
            device_id=dev(x, y, zt, k), device_id_type=MESH,
        )
        return zt != z, cp

    def sum_z_start(h):
        for i in range(4):
            other, cp = sum_z(h, i)
            pl.when(other)(cp.start)

    def all_z(d):
        return pltpu.make_async_remote_copy(
            src_ref=zg.at[z], dst_ref=zg.at[z], send_sem=zsem.at[2, d], recv_sem=zsem.at[3, d],
            device_id=zdev[d], device_id_type=MESH,
        )

    def scale(h):
        @pl.when(z // 4 == h)
        def _():
            diag = lax.broadcasted_iota(jnp.int32, (32, 32), 0) == lax.broadcasted_iota(jnp.int32, (32, 32), 1)
            col = jnp.sum(jnp.where(diag, eo[...], 0.0), axis=1, keepdims=True)
            denom = col * ei[...] + damp[...]
            v = e[z].astype(F32)
            for d in range(1, 8):
                pltpu.make_async_remote_copy(
                    src_ref=e.at[z], dst_ref=re.at[d], send_sem=zsem.at[0, 0], recv_sem=zsem.at[1, d],
                    device_id=zdev[d], device_id_type=MESH,
                ).wait_recv()
            for d in range(1, 8):
                v = v + re[d].astype(F32)
            zg[z] = (v / denom[None]).astype(BF)
            for d in (4, 3, 5, 2, 6, 1, 7):
                all_z(d).start()

    yl = pl.ds(pl.multiple_of(128 * y, 128), 128)
    hl = pl.ds(pl.multiple_of(128 * xh, 128), 128)

    def middle(h):
        for i in range(4):
            zz = 4 * h + i
            d = (z - zz + 8) % 8

            @pl.when(zz != z)
            def _():
                pltpu.make_async_remote_copy(
                    src_ref=zg.at[zz], dst_ref=zg.at[zz], send_sem=zsem.at[2, d], recv_sem=zsem.at[3, d],
                    device_id=zdev[1], device_id_type=MESH,
                ).wait_recv()

        rows = pl.ds(4 * h, 4)
        cps0 = [send(zg.at[rows, 0], st0.at[xh, k, rows, xl, :, yl], ydev[d]) for d in (1, 0, 2)]
        cps1 = [send(zg.at[rows, 1], st1.at[y, k, rows, xl, :, hl], xdev[d]) for d in (1, 0, 2)]
        st0[xh, k, rows, xl, :, yl] = zg[rows, 0]
        st1[y, k, rows, xl, :, hl] = zg[rows, 1]
        return cps0, cps1

    def reg(q, h, v, half=None):
        rows = pl.ds(4 * h, 4) if half is None else pl.ds(4 * h + 2 * half, 2)
        if q == 0:
            return st0.at[v // 2, k, rows, v % 2]
        return st1.at[v, k, rows]

    heavy = {}
    cores = {}

    def wide(q, h, cps):
        for cp in cps:
            cp.wait_recv()
        blk = reg(q, h, x if q == 0 else y)
        to = xdev if q == 0 else ydev
        heavy[q, h] = [send(blk, blk, to[0]), send(blk, blk, to[2])]
        cores[q, h] = [send(blk, blk, sib)]

    def onward(q, h):
        to = xdev if q == 0 else ydev
        at = x if q == 0 else y
        got = heavy[q, h]
        heavy[q, h] = []
        for i in range(2):
            got[i].wait_recv()
            v = (at + 3) % 4 if i == 0 else (at + 1) % 4
            part = reg(q, h, v, i)
            heavy[q, h].append(send(part, part, to[2 * i]))
            blk = reg(q, h, v)
            cores[q, h].append(send(blk, blk, sib))

    def spread(q, h):
        for i in range(2):
            heavy[q, h][i].wait_recv()
            blk = reg(q, h, ((x if q == 0 else y) + 2) % 4, i)
            cores[q, h].append(send(blk, blk, sib))

    outs = []

    def finish(q, h):
        for cp in cores[q, h]:
            cp.wait_recv()
        basis = bi0 if q == 0 else bi1
        rows4 = pl.ds(4 * h, 4)
        for kk in range(2):
            if q == 0:
                s = [st0[n, kk, rows4].reshape(256, 512) for n in range(2)]
            else:
                s = [st1[n, kk, rows4].reshape(256, 256) for n in range(4)]
            s = jnp.concatenate(s, axis=1)
            for m in range(4):
                v = nt(basis[pl.ds(256 * m, 256), :], s).astype(BF)
                yt[q, h, m // 2, :, pl.ds(512 * (m % 2) + 256 * kk, 256)] = v
        for m in range(4):
            rows = pl.ds(256 * m, 256)
            v = yt[q, h, m // 2, :, pl.ds(512 * (m % 2), 512)]
            for lo, width in ((0, 256), (256, 256), (512, 256), (768, 128)):
                cols = pl.ds(lo, width)
                rhs = [bot[kk, rows4, :, cols].reshape(256, width) for kk in range(2)]
                o = nn(v, jnp.concatenate(rhs, axis=0))
                if h == 0:
                    acc[q, rows, cols] = o
                else:
                    ob[q, rows, cols] = (acc[q, rows, cols] + o).astype(BF)
            if h == 1 and m % 2 == 1:
                rows = pl.ds(512 * (m // 2), 512)
                cp = pltpu.make_async_copy(ob.at[q, rows], out_hbm.at[q, rows], lsem.at[6 + 2 * q + m // 2])
                cp.start()
                outs.append(cp)

    firsts = {}
    p0 = partial(0)
    p1 = partial(1)
    firsts[0] = first(0, p0)
    p2 = partial(2)
    firsts[1] = first(1, p1)
    p3 = partial(3)
    r0 = relay(0, 1)
    firsts[2] = first(2, p2)
    r1 = relay(1, 1)
    firsts[3] = first(3, p3)

    eye = (
        lax.broadcasted_iota(jnp.int32, (256, 256), 0) == lax.broadcasted_iota(jnp.int32, (256, 256), 1)
    ).astype(F32).astype(BF)
    for i in range(4):
        for n in range(4):
            v = nt(eye, bit[pl.ds(2 * n, 2), :, :, :, pl.ds(256 * i, 256)].reshape(256, 256)).astype(BF)
            rows = pl.ds(256 * i, 256)
            bi0[rows, pl.ds(256 * n, 256)] = v
            for b in range(2):
                rr = 2 * n + b
                bi1[rows, pl.ds(256 * (rr % 4) + 128 * (rr // 4), 128)] = v[:, 128 * b : 128 * b + 128]
    for cp in later:
        cp.wait()

    s0 = second(0, r0)
    s1 = second(1, r1)
    r2 = relay(2, 1)
    r3 = relay(3, 1)
    third(0, s0)
    third(1, s1)
    sum_z_start(0)
    s2 = second(2, r2)
    s3 = second(3, r3)
    third(2, s2)
    third(3, s3)
    sum_z_start(1)
    scale(0)
    scale(1)
    m0 = middle(0)
    wide(0, 0, m0[0])
    wide(1, 0, m0[1])
    m1 = middle(1)
    onward(0, 0)
    onward(1, 0)
    wide(0, 1, m1[0])
    wide(1, 1, m1[1])
    spread(0, 0)
    spread(1, 0)
    onward(0, 1)
    onward(1, 1)
    finish(0, 0)
    spread(0, 1)
    finish(1, 0)
    spread(1, 1)
    finish(0, 1)
    finish(1, 1)
    for cp in sends:
        cp.wait_send()
    for h in range(2):
        for i in range(4):
            other, cp = sum_z(h, i)
            pl.when(other)(cp.wait_send)
    for d in range(1, 8):
        all_z(d).wait_send()
    for cp in outs:
        cp.wait()
    assert counter[0] <= NSEM, counter[0]


def body(query_grads, basis_in, basis_out, eig_in, eig_out, damping):
    hbm = pl.BlockSpec(memory_space=pl.ANY)
    return pl.pallas_call(
        kernel,
        out_shape=jax.ShapeDtypeStruct((2, 1024, 896), BF),
        in_specs=[pl.BlockSpec(memory_space=pltpu.HBM)] * 6,
        out_specs=hbm,
        scratch_shapes=[
            pltpu.VMEM((2, 1024, 896), BF),
            pltpu.VMEM((896, 128), BF),
            pltpu.VMEM((8, 2, 2, 32, 1024), BF),
            pltpu.VMEM((2, 8, 64, 896), BF),
            pltpu.VMEM((2, 2, 2, 256, 1024), BF),
            pltpu.VMEM((4, 256, 1024), BF),
            pltpu.VMEM((4, 256, 1024), BF),
            pltpu.VMEM((4, 256, 1024), F32),
            pltpu.VMEM((2, 4, 128, 512), BF),
            pltpu.VMEM((2, 4, 512, 128), BF),
            pltpu.VMEM((2, 3, 128, 512), BF),
            pltpu.VMEM((2, 3, 512, 128), BF),
            pltpu.VMEM((2, 4, 128, 128), BF),
            pltpu.VMEM((2, 4, 128, 128), BF),
            pltpu.VMEM((2, 3, 128, 128), BF),
            pltpu.VMEM((2, 3, 128, 128), BF),
            pltpu.VMEM((8, 2, 32, 128), BF),
            pltpu.VMEM((8, 2, 32, 128), BF),
            pltpu.VMEM((8, 2, 32, 128), BF),
            pltpu.VMEM((2, 2, 8, 2, 32, 512), BF),
            pltpu.VMEM((4, 2, 8, 2, 32, 256), BF),
            pltpu.VMEM((1024, 1024), BF),
            pltpu.VMEM((1024, 1024), BF),
            pltpu.VMEM((2, 1024, 896), F32),
            pltpu.VMEM((2, 1024, 896), BF),
            pltpu.VMEM((1, 128), F32),
            pltpu.VMEM((1, 32), F32),
            pltpu.VMEM((1, 1), F32),
            pltpu.SemaphoreType.DMA((NSEM,)),
            pltpu.SemaphoreType.DMA((NSEM,)),
            pltpu.SemaphoreType.DMA((10,)),
            pltpu.SemaphoreType.DMA((4, 8)),
        ],
        compiler_params=pltpu.CompilerParams(
            collective_id=1, has_side_effects=True, vmem_limit_bytes=VMEM
        ),
        cost_estimate=pl.CostEstimate(flops=17_000_000_000, bytes_accessed=8_000_000, transcendentals=0),
    )(
        query_grads,
        *(
            pltpu.with_memory_space_constraint(v, pltpu.HBM)
            for v in (basis_in.T, basis_out, eig_in.reshape(1, 128), eig_out.reshape(1, 32))
        ),
        damping.reshape(1, 1),
    )


def solution(mesh):
    return jax.shard_map(
        body,
        mesh=mesh,
        in_specs=(P(None, "row", "col"), P("row", "col"), P("col", "row"), P("row"), P("col"), P()),
        out_specs=P(None, "row", "col"),
        check_vma=False,
    )
```

```python
import functools

import jax
import jax.numpy as jnp
from jax import lax
from jax.experimental import pallas as pl
from jax.experimental.pallas import tpu as pltpu
from jax.sharding import PartitionSpec as P

MESH = pl.DeviceIdType.MESH
BF = jnp.bfloat16
F32 = jnp.float32
NSEM = 224
VMEM = 49152 * 1024


def nt(a, b):
    return lax.dot_general(a, b, (((1,), (1,)), ((), ())), preferred_element_type=F32)


def nn(a, b):
    return lax.dot_general(a, b, (((1,), (0,)), ((), ())), preferred_element_type=F32)


def kernel(
    g_hbm, bi_hbm, bo_hbm, ei_hbm, eo_hbm, damp_hbm, out_hbm,
    g, bov, bit, bot, yt, sibs, sibr, own, c1a, c1b, r1a, r1b, c2a, c2b, r2a, r2b, e, re, zg,
    st0, st1, bi0, bi1, acc, ob, ei, eo, damp, ssem, rsem, lsem, zsem,
):
    r = lax.axis_index("row")
    c = lax.axis_index("col")
    xh, y, z, xl, k = r // 4, r % 4, c // 4, (c // 2) % 2, c % 2
    x = 2 * xh + xl

    def dev(x_, y_, z_, k_):
        return ((x_ // 2) * 4 + y_, z_ * 4 + (x_ % 2) * 2 + k_)

    xs = [(x + d) % 4 for d in (1, 2, 3)]
    ys = [(y + d) % 4 for d in (1, 2, 3)]
    xdev = [dev(v, y, z, k) for v in xs]
    ydev = [dev(x, v, z, k) for v in ys]
    zdev = [None] + [dev(x, y, (z + d) % 8, k) for d in range(1, 8)]
    sib = dev(x, y, z, 1 - k)
    xlp = dev(2 * xh + 1 - xl, y, z, k)
    xhp = xdev[1]

    sends = []
    counter = [0]

    def send(src, dst, to):
        i = counter[0]
        counter[0] += 1
        cp = pltpu.make_async_remote_copy(
            src_ref=src, dst_ref=dst, send_sem=ssem.at[i], recv_sem=rsem.at[i],
            device_id=to, device_id_type=MESH,
        )
        cp.start()
        sends.append(cp)
        return cp

    def load(i, src, dst):
        cp = pltpu.make_async_copy(src, dst, lsem.at[i])
        cp.start()
        return cp

    barrier = pltpu.get_barrier_semaphore()
    partners = [xdev[1], xdev[0], xdev[2], ydev[0], ydev[2], zdev[1], zdev[7], sib]
    for p in partners:
        pl.semaphore_signal(barrier, inc=1, device_id=p, device_id_type=MESH)
    lbo = load(0, bo_hbm, bov)
    lbi = load(1, bi_hbm, bit.at[z, xl, k])
    later = [load(2, ei_hbm, ei), load(3, eo_hbm, eo), load(4, damp_hbm, damp)]
    lg = load(5, g_hbm, g)

    lbo.wait()
    to = lax.broadcasted_iota(jnp.int32, (128, 128), 0)
    at = (to // 32 % 2) * 64 + (to // 64) * 32 + to % 32
    perm = (at == lax.broadcasted_iota(jnp.int32, (128, 128), 1)).astype(F32).astype(BF)
    v = nt(perm, bov[...]).astype(BF)
    bot[0, r] = v[:64]
    bot[1, r] = v[64:]
    lbi.wait()
    pl.semaphore_wait(barrier, len(partners))

    yup, ydn = ydev[0], ydev[2]
    zr, zl = zdev[1], zdev[7]
    me = bit.at[z, xl, k]
    ring = {(0, 0, 1): send(me, me, zr), (1, 0, 1): send(me, me, zl)}
    bi_x = send(me, me, xlp)
    blk = bot.at[0, r]
    a_x = send(blk, blk, xhp)
    near = {}
    blk = bot.at[1, r]
    near[1, "own"] = [send(blk, blk, yup), send(blk, blk, ydn)]
    bi_sib = [send(me, me, sib)]

    def pass_y(kk, side, hh):
        for cp in near[kk, side]:
            cp.wait_recv()
        lo = bot.at[kk, 4 * hh + (y + 3) % 4, pl.ds(0, 32)]
        hi = bot.at[kk, 4 * hh + (y + 1) % 4, pl.ds(32, 32)]
        near[kk, side, 2] = [send(lo, lo, yup), send(hi, hi, ydn)]

    def ring_step(t, b):
        for d in range(2):
            if (d, b, t) not in ring:
                continue
            ring[d, b, t].wait_recv()
            zz = (z - t + 8) % 8 if d == 0 else (z + t) % 8
            blk = bit.at[zz, xl if b == 0 else 1 - xl, k]
            if t < 3 or (t == 3 and b == d):
                ring[d, b, t + 1] = send(blk, blk, zr if d == 0 else zl)
            bi_sib.append(send(blk, blk, sib))

    def y_dot(kk, h, q):
        lhs = bot[kk, pl.ds(4 * h, 4)].reshape(256, 896)
        for n in range(2):
            yt[kk, h, q, :, pl.ds(512 * n, 512)] = nt(lhs, g[q, pl.ds(512 * n, 512), :]).astype(BF)

    bi_x.wait_recv()
    blk = bit.at[z, 1 - xl, k]
    ring[0, 1, 1] = send(blk, blk, zr)
    ring[1, 1, 1] = send(blk, blk, zl)
    blk = bot.at[1, r]
    b_x = [send(blk, blk, xhp)]
    blk = bit.at[z, 1 - xl, k]
    bi_sib.append(send(blk, blk, sib))
    pass_y(1, "own", xh)
    for v in ((y + 3) % 4, (y + 1) % 4):
        blk = bot.at[1, 4 * xh + v]
        b_x.append(send(blk, blk, xhp))
    blk = bot.at[0, r]
    near[0, "own"] = [send(blk, blk, yup), send(blk, blk, ydn)]
    ring_step(1, 0)
    for i, cp in enumerate(near[1, "own", 2]):
        cp.wait_recv()
        blk = bot.at[1, 4 * xh + (y + 2) % 4, pl.ds(32 * i, 32)]
        b_x.append(send(blk, blk, xhp))
    a_x.wait_recv()
    blk = bot.at[0, 4 * (1 - xh) + y]
    near[0, "far"] = [send(blk, blk, yup), send(blk, blk, ydn)]
    ring_step(1, 1)
    ring_step(2, 0)
    pass_y(0, "own", xh)
    pass_y(0, "far", 1 - xh)
    ring_step(2, 1)
    ring_step(3, 0)
    lg.wait()
    y_dot(1, xh, 0)
    y_dot(1, xh, 1)
    ring_step(3, 1)
    ring_step(4, 0)
    for cp in near[0, "own", 2]:
        cp.wait_recv()
    y_dot(0, xh, 0)
    y_dot(0, xh, 1)
    ring_step(4, 1)
    for cp in near[0, "far", 2]:
        cp.wait_recv()
    y_dot(0, 1 - xh, 0)
    y_dot(0, 1 - xh, 1)
    for cp in b_x:
        cp.wait_recv()
    y_dot(1, 1 - xh, 0)
    y_dot(1, 1 - xh, 1)
    for cp in bi_sib:
        cp.wait_recv()

    chunks = [(0, 0), (1, 0), (0, 1), (1, 1)]

    def bit_cols(n):
        return bit[pl.ds(2 * n, 2)].reshape(256, 1024)

    def partial(i):
        q, h = chunks[i]
        lhs = yt[1 - k, h, q]
        for n in range(4):
            sibs[i, :, pl.ds(256 * n, 256)] = nt(lhs, bit_cols(n)).astype(BF)
        cp = send(sibs.at[i], sibr.at[i], sib)
        lhs = yt[k, h, q]
        for n in range(4):
            own[i, :, pl.ds(256 * n, 256)] = nt(lhs, bit_cols(n))
        return cp

    def first(i, cp):
        q, h = chunks[i]
        cp.wait_recv()
        for zz in range(4):
            for xx in range(2):
                rows = pl.ds(64 * zz + 32 * xx, 32)
                v = (own[i, rows, :] + sibr[i, rows, :].astype(F32)).astype(BF)
                if q == 0:
                    for hh in range(2):
                        c1a[h, 2 * hh + xx, pl.ds(32 * zz, 32), :] = v[:, 512 * hh : 512 * hh + 512]
                else:
                    for hh in range(2):
                        for yy in range(4):
                            lo = 512 * hh + 128 * yy
                            c1b[h, yy, pl.ds(128 * (2 * hh + xx) + 32 * zz, 32), :] = v[:, lo : lo + 128]
        return relay(i, 0)

    def relay(i, step):
        q, h = chunks[i]
        src, dst, n, at = (c1a, r1a, 64, x) if q == 0 else (c1b, r1b, 256, y)
        far, up, down = (at + 2) % 4, (at + 1) % 4, (at + 3) % 4
        pu, _, pd = xdev if q == 0 else ydev
        lo, hi = pl.ds(0, n), pl.ds(n, n)
        if step == 0:
            return [
                send(src.at[h, far, lo], dst.at[h, 0, lo], pu),
                send(src.at[h, far, hi], dst.at[h, 0, hi], pd),
                send(src.at[h, up, hi], dst.at[h, 1, hi], pu),
                send(src.at[h, down, lo], dst.at[h, 2, lo], pd),
            ]
        cps = firsts[i]
        cps[0].wait_recv()
        src[h, up, lo, :] = (src[h, up, lo, :].astype(F32) + dst[h, 0, lo, :].astype(F32)).astype(BF)
        a = send(src.at[h, up, lo], dst.at[h, 1, lo], pu)
        cps[1].wait_recv()
        src[h, down, hi, :] = (src[h, down, hi, :].astype(F32) + dst[h, 0, hi, :].astype(F32)).astype(BF)
        b = send(src.at[h, down, hi], dst.at[h, 2, hi], pd)
        return [cps[2], cps[3], a, b]

    def second(i, cps):
        q, h = chunks[i]
        for cp in cps:
            cp.wait_recv()
        if q == 0:
            for zz in range(4):
                rows = pl.ds(32 * zz, 32)
                v = c1a[h, x, rows, :].astype(F32)
                for d in range(1, 3):
                    v = v + r1a[h, d, rows, :].astype(F32)
                v = v.astype(BF)
                for yy in range(4):
                    c2a[h, yy, rows, :] = v[:, 128 * yy : 128 * yy + 128]
            return [send(c2a.at[h, ys[d]], r2a.at[h, d], ydev[d]) for d in (1, 0, 2)]
        for xx in range(4):
            rows = pl.ds(128 * xx, 128)
            v = c1b[h, y, rows, :].astype(F32)
            for d in range(1, 3):
                v = v + r1b[h, d, rows, :].astype(F32)
            c2b[h, xx] = v.astype(BF)
        return [send(c2b.at[h, xs[d]], r2b.at[h, d], xdev[d]) for d in (1, 0, 2)]

    def third(i, cps):
        q, h = chunks[i]
        for cp in cps:
            cp.wait_recv()
        if q == 0:
            v = c2a[h, y].astype(F32)
            for d in range(3):
                v = v + r2a[h, d].astype(F32)
        else:
            v = c2b[h, x].astype(F32)
            for d in range(3):
                v = v + r2b[h, d].astype(F32)
        v = v.astype(BF)
        for zz in range(4):
            e[4 * h + zz, q] = v[32 * zz : 32 * zz + 32, :]

    def sum_z(h, i):
        zt = 4 * h + i
        d = (zt - z + 8) % 8
        cp = pltpu.make_async_remote_copy(
            src_ref=e.at[zt], dst_ref=re.at[d], send_sem=zsem.at[0, zt], recv_sem=zsem.at[1, d],
            device_id=dev(x, y, zt, k), device_id_type=MESH,
        )
        return zt != z, cp

    def sum_z_start(h):
        for i in range(4):
            other, cp = sum_z(h, i)
            pl.when(other)(cp.start)

    def all_z(d):
        return pltpu.make_async_remote_copy(
            src_ref=zg.at[z], dst_ref=zg.at[z], send_sem=zsem.at[2, d], recv_sem=zsem.at[3, d],
            device_id=zdev[d], device_id_type=MESH,
        )

    def scale(h):
        @pl.when(z // 4 == h)
        def _():
            diag = lax.broadcasted_iota(jnp.int32, (32, 32), 0) == lax.broadcasted_iota(jnp.int32, (32, 32), 1)
            col = jnp.sum(jnp.where(diag, eo[...], 0.0), axis=1, keepdims=True)
            denom = col * ei[...] + damp[...]
            v = e[z].astype(F32)
            for d in range(1, 8):
                pltpu.make_async_remote_copy(
                    src_ref=e.at[z], dst_ref=re.at[d], send_sem=zsem.at[0, 0], recv_sem=zsem.at[1, d],
                    device_id=zdev[d], device_id_type=MESH,
                ).wait_recv()
            for d in range(1, 8):
                v = v + re[d].astype(F32)
            zg[z] = (v / denom[None]).astype(BF)
            for d in (4, 3, 5, 2, 6, 1, 7):
                all_z(d).start()

    yl = pl.ds(pl.multiple_of(128 * y, 128), 128)
    hl = pl.ds(pl.multiple_of(128 * xh, 128), 128)

    def middle(h):
        for i in range(4):
            zz = 4 * h + i
            d = (z - zz + 8) % 8

            @pl.when(zz != z)
            def _():
                pltpu.make_async_remote_copy(
                    src_ref=zg.at[zz], dst_ref=zg.at[zz], send_sem=zsem.at[2, d], recv_sem=zsem.at[3, d],
                    device_id=zdev[1], device_id_type=MESH,
                ).wait_recv()

        rows = pl.ds(4 * h, 4)
        cps0 = [send(zg.at[rows, 0], st0.at[xh, k, rows, xl, :, yl], ydev[d]) for d in (1, 0, 2)]
        cps1 = [send(zg.at[rows, 1], st1.at[y, k, rows, xl, :, hl], xdev[d]) for d in (1, 0, 2)]
        st0[xh, k, rows, xl, :, yl] = zg[rows, 0]
        st1[y, k, rows, xl, :, hl] = zg[rows, 1]
        return cps0, cps1

    def reg(q, h, v, half=None):
        rows = pl.ds(4 * h, 4) if half is None else pl.ds(4 * h + 2 * half, 2)
        if q == 0:
            return st0.at[v // 2, k, rows, v % 2]
        return st1.at[v, k, rows]

    heavy = {}
    cores = {}

    def wide(q, h, cps):
        for cp in cps:
            cp.wait_recv()
        blk = reg(q, h, x if q == 0 else y)
        to = xdev if q == 0 else ydev
        a, b = [reg(q, h, x if q == 0 else y, i) for i in range(2)]
        heavy[q, h] = [send(a, a, to[0]), send(b, b, to[2]), send(b, b, to[0]), send(a, a, to[2])]
        cores[q, h] = [send(blk, blk, sib)]

    def onward(q, h):
        to = xdev if q == 0 else ydev
        at = x if q == 0 else y
        for i in range(2):
            heavy[q, h][i].wait_recv()
            blk = reg(q, h, (at + 3) % 4 if i == 0 else (at + 1) % 4, i)
            heavy[q, h].append(send(blk, blk, to[2 * i]))
            cores[q, h].append(send(blk, blk, sib))

    def spread(q, h):
        at = x if q == 0 else y
        for n, v, i in ((2, at + 3, 1), (3, at + 1, 0), (4, at + 2, 0), (5, at + 2, 1)):
            heavy[q, h][n].wait_recv()
            blk = reg(q, h, v % 4, i)
            cores[q, h].append(send(blk, blk, sib))

    outs = []

    def finish(q, h):
        for cp in cores[q, h]:
            cp.wait_recv()
        basis = bi0 if q == 0 else bi1
        rows4 = pl.ds(4 * h, 4)
        for kk in range(2):
            if q == 0:
                s = [st0[n, kk, rows4].reshape(256, 512) for n in range(2)]
            else:
                s = [st1[n, kk, rows4].reshape(256, 256) for n in range(4)]
            s = jnp.concatenate(s, axis=1)
            for m in range(4):
                v = nt(basis[pl.ds(256 * m, 256), :], s).astype(BF)
                yt[q, h, m // 2, :, pl.ds(512 * (m % 2) + 256 * kk, 256)] = v
        for m in range(4):
            rows = pl.ds(256 * m, 256)
            v = yt[q, h, m // 2, :, pl.ds(512 * (m % 2), 512)]
            for lo, width in ((0, 256), (256, 256), (512, 256), (768, 128)):
                cols = pl.ds(lo, width)
                rhs = [bot[kk, rows4, :, cols].reshape(256, width) for kk in range(2)]
                o = nn(v, jnp.concatenate(rhs, axis=0))
                if h == 0:
                    acc[q, rows, cols] = o
                else:
                    ob[q, rows, cols] = (acc[q, rows, cols] + o).astype(BF)
            if h == 1 and m % 2 == 1:
                rows = pl.ds(512 * (m // 2), 512)
                cp = pltpu.make_async_copy(ob.at[q, rows], out_hbm.at[q, rows], lsem.at[6 + 2 * q + m // 2])
                cp.start()
                outs.append(cp)

    firsts = {}
    p0 = partial(0)
    p1 = partial(1)
    firsts[0] = first(0, p0)
    p2 = partial(2)
    firsts[1] = first(1, p1)
    p3 = partial(3)
    r0 = relay(0, 1)
    firsts[2] = first(2, p2)
    r1 = relay(1, 1)
    firsts[3] = first(3, p3)

    eye = (
        lax.broadcasted_iota(jnp.int32, (256, 256), 0) == lax.broadcasted_iota(jnp.int32, (256, 256), 1)
    ).astype(F32).astype(BF)
    for i in range(4):
        for n in range(4):
            v = nt(eye, bit[pl.ds(2 * n, 2), :, :, :, pl.ds(256 * i, 256)].reshape(256, 256)).astype(BF)
            rows = pl.ds(256 * i, 256)
            bi0[rows, pl.ds(256 * n, 256)] = v
            for b in range(2):
                rr = 2 * n + b
                bi1[rows, pl.ds(256 * (rr % 4) + 128 * (rr // 4), 128)] = v[:, 128 * b : 128 * b + 128]
    for cp in later:
        cp.wait()

    s0 = second(0, r0)
    s1 = second(1, r1)
    r2 = relay(2, 1)
    r3 = relay(3, 1)
    third(0, s0)
    third(1, s1)
    sum_z_start(0)
    s2 = second(2, r2)
    s3 = second(3, r3)
    third(2, s2)
    third(3, s3)
    sum_z_start(1)
    scale(0)
    scale(1)
    m0 = middle(0)
    wide(0, 0, m0[0])
    wide(1, 0, m0[1])
    m1 = middle(1)
    onward(0, 0)
    onward(1, 0)
    wide(0, 1, m1[0])
    wide(1, 1, m1[1])
    spread(0, 0)
    spread(1, 0)
    onward(0, 1)
    finish(0, 0)
    onward(1, 1)
    spread(0, 1)
    finish(1, 0)
    spread(1, 1)
    finish(0, 1)
    finish(1, 1)
    for cp in sends:
        cp.wait_send()
    for h in range(2):
        for i in range(4):
            other, cp = sum_z(h, i)
            pl.when(other)(cp.wait_send)
    for d in range(1, 8):
        all_z(d).wait_send()
    for cp in outs:
        cp.wait()
    assert counter[0] <= NSEM, counter[0]


def body(query_grads, basis_in, basis_out, eig_in, eig_out, damping):
    hbm = pl.BlockSpec(memory_space=pl.ANY)
    return pl.pallas_call(
        kernel,
        out_shape=jax.ShapeDtypeStruct((2, 1024, 896), BF),
        in_specs=[pl.BlockSpec(memory_space=pltpu.HBM)] * 6,
        out_specs=hbm,
        scratch_shapes=[
            pltpu.VMEM((2, 1024, 896), BF),
            pltpu.VMEM((896, 128), BF),
            pltpu.VMEM((8, 2, 2, 32, 1024), BF),
            pltpu.VMEM((2, 8, 64, 896), BF),
            pltpu.VMEM((2, 2, 2, 256, 1024), BF),
            pltpu.VMEM((4, 256, 1024), BF),
            pltpu.VMEM((4, 256, 1024), BF),
            pltpu.VMEM((4, 256, 1024), F32),
            pltpu.VMEM((2, 4, 128, 512), BF),
            pltpu.VMEM((2, 4, 512, 128), BF),
            pltpu.VMEM((2, 3, 128, 512), BF),
            pltpu.VMEM((2, 3, 512, 128), BF),
            pltpu.VMEM((2, 4, 128, 128), BF),
            pltpu.VMEM((2, 4, 128, 128), BF),
            pltpu.VMEM((2, 3, 128, 128), BF),
            pltpu.VMEM((2, 3, 128, 128), BF),
            pltpu.VMEM((8, 2, 32, 128), BF),
            pltpu.VMEM((8, 2, 32, 128), BF),
            pltpu.VMEM((8, 2, 32, 128), BF),
            pltpu.VMEM((2, 2, 8, 2, 32, 512), BF),
            pltpu.VMEM((4, 2, 8, 2, 32, 256), BF),
            pltpu.VMEM((1024, 1024), BF),
            pltpu.VMEM((1024, 1024), BF),
            pltpu.VMEM((2, 1024, 896), F32),
            pltpu.VMEM((2, 1024, 896), BF),
            pltpu.VMEM((1, 128), F32),
            pltpu.VMEM((1, 32), F32),
            pltpu.VMEM((1, 1), F32),
            pltpu.SemaphoreType.DMA((NSEM,)),
            pltpu.SemaphoreType.DMA((NSEM,)),
            pltpu.SemaphoreType.DMA((10,)),
            pltpu.SemaphoreType.DMA((4, 8)),
        ],
        compiler_params=pltpu.CompilerParams(
            collective_id=1, has_side_effects=True, vmem_limit_bytes=VMEM
        ),
        cost_estimate=pl.CostEstimate(flops=17_000_000_000, bytes_accessed=8_000_000, transcendentals=0),
    )(
        query_grads,
        *(
            pltpu.with_memory_space_constraint(v, pltpu.HBM)
            for v in (basis_in.T, basis_out, eig_in.reshape(1, 128), eig_out.reshape(1, 32))
        ),
        damping.reshape(1, 1),
    )


def solution(mesh):
    return jax.shard_map(
        body,
        mesh=mesh,
        in_specs=(P(None, "row", "col"), P("row", "col"), P("col", "row"), P("row"), P("col"), P()),
        out_specs=P(None, "row", "col"),
        check_vma=False,
    )
```
